256 devices in a mesh: expert: 16 (over x, y_hi, core), edp: 16 (over y_lo, z).
Axes of the slice: x: 4, y: 4 (y_hi: 2, y_lo: 2; y = y_hi * 2 + y_lo), z: 8, core: 2. Of those that a mesh axis runs over, the one named last changes fastest.
Arguments:
- master: float32 [16, 1024, 3584], P('expert', 'edp'), may hold values from -0.1875 to 0.1875
- moment_one: bfloat16 [16, 1024, 3584], P('expert', 'edp'), may hold values from -4 to 4
- moment_two: bfloat16 [16, 1024, 3584], P('expert', 'edp'), may hold values from 0.049804688 to 2
- hidden_saved: bfloat16 [16, 16, 768, 1024], P('expert', 'edp'), may hold values from -6 to 6
- out_grad: bfloat16 [16, 16, 768, 3584], P('expert', 'edp'), may hold values from -0.078125 to 0.078125
- counts: int32 [16, 16, 16], replicated, may hold values from 0 to 48, as said below
- next_hidden: bfloat16 [16, 4096, 1024], P('expert', 'edp'), may hold values from -6 to 6
Outputs:
- new_master: float32 [16, 1024, 3584], P('expert', 'edp')
- new_moment_one: bfloat16 [16, 1024, 3584], P('expert', 'edp')
- new_moment_two: bfloat16 [16, 1024, 3584], P('expert', 'edp')
- next_out: bfloat16 [16, 4096, 3584], P('expert', 'edp')
The draws below stay inside these ranges and needn't reach their ends.
Inputs may be any that keep to these rules, and one draw needn't show every extreme that they name: `counts`: for every edp index some expert receives 48 rows from every source, and every pair of edp index and expert receives 48 rows from at least one source.
All inputs are finite; a program needn't handle non-finite values.
Results may differ from the reference program's by a relative error of at most 0.0049.
Values may be sent and summed in bfloat16 or wider, within the bound.
No kernel may reach another device: no remote copies, remote signals or barrier semaphores. Data moves between devices by JAX's collectives and lax.ppermute only.
A program may use at most 128 MiB of HBM per device.

```python
import math
import jax
import jax.numpy as jnp
from jax import lax

D_W = 3584
FF_W = 1024
ROWS_DEV = 768
EXPERTS = 16
CAPS = 48
NEXT_DEV = 256
N_EDP = 16


def draw_counts(key, part):
    key = jax.random.fold_in(key, 11)
    key_appetite, key_base, key_source, key_target = jax.random.split(key, 4)
    appetite = jax.random.randint(key_appetite, (1, N_EDP, EXPERTS), 1, 9)
    base = jax.random.randint(key_base, (EXPERTS, N_EDP, EXPERTS), 0, CAPS + 1)
    drawn = jnp.minimum(CAPS, base * appetite // 4)
    full_source = jax.random.randint(key_source, (1, N_EDP, EXPERTS), 0, EXPERTS)
    source_ids = jnp.arange(EXPERTS).reshape(EXPERTS, 1, 1)
    drawn = jnp.where(source_ids == full_source, CAPS, drawn)
    busy_target = jax.random.randint(key_target, (1, N_EDP, 1), 0, EXPERTS)
    target_ids = jnp.arange(EXPERTS).reshape(1, 1, EXPERTS)
    drawn = jnp.where(target_ids == busy_target, CAPS, drawn)
    return drawn.astype(jnp.int32)


def level_of(key, extent, shards, least, largest):
    factor_of = 1.0
    for position, parts in shards:
        heights = jax.random.uniform(jax.random.fold_in(jax.random.fold_in(key, 6), position), (parts,), jnp.float32, least / len(shards), largest / len(shards))
        factor_of = factor_of * jnp.repeat(jnp.exp(heights), extent[position] // parts).reshape((-1,) + (1,) * (len(extent) - 1 - position))
    return factor_of


def gaussian(key, shape, deviation, limit, cuts=(), kind=jnp.bfloat16):
    entries = deviation * jax.random.normal(key, shape, jnp.float32)
    if cuts:
        entries = entries * level_of(key, shape, cuts, -0.22, 0.18)
    return jnp.clip(entries, -limit, limit).astype(kind)


def setup_inputs(seed: int = 0) -> dict:
    arg_keys = jax.random.split(jax.random.key(seed), 8)
    master = gaussian(arg_keys[0], (EXPERTS, FF_W, D_W), FF_W ** -0.5, 0.1875, ((0, 16), (1, 16)), jnp.float32)
    moment_one = gaussian(arg_keys[1], (EXPERTS, FF_W, D_W), 0.3, 4.0, ((0, 16), (1, 16)))
    moment_two = jnp.clip(jnp.exp(math.log(2.0) - 3.6927934 * jax.random.uniform(arg_keys[2], (EXPERTS, FF_W, D_W), jnp.float32) ** level_of(arg_keys[2], (EXPERTS, FF_W, D_W), ((0, 16), (1, 16)), -0.2, 0.2)), 0.049804688, 2.0).astype(jnp.bfloat16)
    hidden_saved = gaussian(arg_keys[3], (EXPERTS, N_EDP, ROWS_DEV, FF_W), 1.0, 6.0, ((0, 16), (1, 16)))
    out_grad = gaussian(arg_keys[4], (EXPERTS, N_EDP, ROWS_DEV, D_W), (N_EDP * ROWS_DEV // 2) ** -0.5, 0.078125, ((0, 16), (1, 16)))
    counts = draw_counts(jax.random.fold_in(arg_keys[7], 71), 0)
    next_hidden = gaussian(arg_keys[6], (EXPERTS, N_EDP * NEXT_DEV, FF_W), 1.0, 6.0, ((0, 16), (1, 16)))
    return {"master": master, "moment_one": moment_one, "moment_two": moment_two, "hidden_saved": hidden_saved, "out_grad": out_grad, "counts": counts, "next_hidden": next_hidden}


learn_rate = 0.002
beta_first = 0.9
beta_second = 0.95
epsilon = 1e-08
decay_rate = 0.1
correct_first = 1.0 - 0.9 ** 10
correct_second = 1.0 - 0.95 ** 10

def reference(master, moment_one, moment_two, hidden_saved, out_grad, counts, next_hidden):
    slot_ids = jnp.arange(CAPS, dtype=jnp.int32)

    def one_expert(expert):
        grads = lax.dynamic_slice_in_dim(out_grad, expert * CAPS, CAPS, 2)
        grads = jnp.transpose(grads, (1, 0, 2, 3)).reshape(N_EDP * ROWS_DEV, D_W)
        given = lax.dynamic_index_in_dim(counts, expert, 2, keepdims=False)
        live_rows = slot_ids[None, None, :] < jnp.transpose(given)[:, :, None]
        hidden = lax.dynamic_index_in_dim(hidden_saved, expert, 0, keepdims=False)
        hidden = jnp.where(live_rows.reshape(N_EDP, ROWS_DEV, 1), hidden, jnp.zeros_like(hidden))
        hidden = hidden.reshape(N_EDP * ROWS_DEV, FF_W)
        gradient = lax.dot_general(hidden, grads, (((0,), (0,)), ((), ())), preferred_element_type=jnp.float32)
        weights_old = lax.dynamic_index_in_dim(master, expert, 0, keepdims=False)
        first_old = lax.dynamic_index_in_dim(moment_one, expert, 0, keepdims=False).astype(jnp.float32)
        second_old = lax.dynamic_index_in_dim(moment_two, expert, 0, keepdims=False).astype(jnp.float32)
        first = beta_first * first_old + (1.0 - beta_first) * gradient
        second = beta_second * second_old + (1.0 - beta_second) * gradient * gradient
        step_size = first / correct_first / (jnp.sqrt(second / correct_second) + epsilon)
        updated = weights_old - learn_rate * (step_size + decay_rate * weights_old)
        weights = updated.astype(jnp.bfloat16)
        upcoming = lax.dynamic_index_in_dim(next_hidden, expert, 0, keepdims=False)
        produced = jnp.dot(upcoming, weights, preferred_element_type=jnp.float32).astype(jnp.bfloat16)
        return (updated, first.astype(jnp.bfloat16), second.astype(jnp.bfloat16), produced)
    results = lax.map(one_expert, jnp.arange(EXPERTS, dtype=jnp.int32))
    return (results[0], results[1], results[2], results[3])
```

```python
import jax
import jax.numpy as jnp
from jax import lax
from jax.sharding import Mesh, PartitionSpec as P

CHUNKS = (5, 5, 4)

learn_rate = 0.002
beta_first = 0.9
beta_second = 0.95
epsilon = 1e-08
decay_rate = 0.1
correct_first = 1.0 - 0.9**10
correct_second = 1.0 - 0.95**10

EXPERT = ("x", "yh", "core")
RING = 8
SWAP = [(0, 1), (1, 0)]
RIGHT = [(i, (i + 1) % RING) for i in range(RING)]
LEFT = [(i, (i - 1) % RING) for i in range(RING)]


def swap(value):
    return lax.ppermute(value, "yl", SWAP)


def to_right(value):
    return lax.ppermute(value, "z", RIGHT)


def to_left(value):
    return lax.ppermute(value, "z", LEFT)


def rolled(value, axis, shift):
    twice = jnp.concatenate([value, value], axis=axis)
    return lax.dynamic_slice_in_dim(twice, shift, RING, axis)


def pick(pair, which):
    return jnp.where(which == 0, pair[0], pair[1])


def reduce_ring(blocks):
    half = blocks.dtype
    bf = jnp.bfloat16
    right = to_right(blocks[4][:1].astype(bf))
    left = to_left(blocks[4][1:].astype(bf))
    f = jnp.float32
    right = to_right(
        jnp.concatenate([blocks[3][:1] + right.astype(f), blocks[3][1:]], 0).astype(bf)
    )
    left = to_left(
        jnp.concatenate([blocks[5][:1], blocks[5][1:] + left.astype(f)], 0).astype(bf)
    )
    for step in (2, 1):
        right = to_right((blocks[step] + right.astype(f)).astype(bf))
        left = to_left((blocks[8 - step] + left.astype(f)).astype(bf))
    return blocks[0] + (right.astype(f) + left.astype(f))


def gather_ring(block):
    right = [block]
    left = [block]
    for _ in range(3):
        right.append(to_right(right[-1]))
        left.append(to_left(left[-1]))
    far = jnp.concatenate([to_right(right[-1][:1]), to_left(left[-1][1:])], 0)
    return [block, left[1], left[2], left[3], far, right[3], right[2], right[1]]


def per_device(master, moment_one, moment_two, hidden_saved, out_grad, counts, next_hidden):
    bf = jnp.bfloat16
    f32 = jnp.float32
    me_expert = lax.axis_index(EXPERT)
    me_half = lax.axis_index("yl")
    me_z = lax.axis_index("z")
    experts = counts.shape[0]
    rows = hidden_saved.shape[2]
    slots = rows // experts
    ff = hidden_saved.shape[3]
    shard = master.shape[1]

    hidden = hidden_saved[0, 0]
    other = swap(hidden)
    loads = lax.dynamic_index_in_dim(counts, me_expert, 2, keepdims=False)
    loads = loads.reshape(experts, 2, RING)
    loads = lax.dynamic_index_in_dim(loads, me_z, 2, keepdims=False).T
    live = jnp.arange(slots, dtype=jnp.int32)[None, None, :] < loads[:, :, None]
    both = jnp.concatenate([pick((hidden, other), me_half), pick((other, hidden), me_half)], 0)
    both = jnp.where(live.reshape(2 * rows, 1), both, jnp.zeros_like(both))
    turned = both.T.reshape(2, RING, shard, 2 * rows)
    turned = rolled(turned, 1, me_z).swapaxes(0, 1).reshape(ff, 2 * rows)

    mine = next_hidden[0]
    upcoming = jnp.concatenate([mine, swap(mine)], 0)
    next_rows = mine.shape[0]
    upcoming = upcoming.reshape(2 * next_rows, 2, RING, shard)
    upcoming = rolled(upcoming, 2, me_z).swapaxes(1, 2).reshape(2 * next_rows, ff)

    grads = out_grad[0, 0]
    new_master, new_one, new_two, outs = [], [], [], []
    begin = 0
    for tiles in CHUNKS:
        w = tiles * 128
        cols = slice(begin, begin + 2 * w)
        part = grads[:, cols].reshape(rows, 2, w).swapaxes(0, 1)
        part = part.reshape(2 * experts, slots, w)
        arrived = lax.all_to_all(part, ("yl",) + EXPERT, 0, 0).reshape(2 * rows, w)
        product = jnp.dot(turned, arrived, preferred_element_type=f32)
        total = reduce_ring(product.reshape(RING, 2, shard, w))
        theirs = swap(pick((total[1], total[0]), me_half).astype(bf)).astype(f32)
        ours = pick((total[0], total[1]), me_half)
        gradient = jnp.concatenate(
            [pick((ours, theirs), me_half), pick((theirs, ours), me_half)], 1
        )
        weights_old = master[0, :, cols]
        first = beta_first * moment_one[0, :, cols].astype(f32) + (1.0 - beta_first) * gradient
        second = (
            beta_second * moment_two[0, :, cols].astype(f32)
            + (1.0 - beta_second) * gradient * gradient
        )
        step_size = first / correct_first / (jnp.sqrt(second / correct_second) + epsilon)
        updated = weights_old - learn_rate * (step_size + decay_rate * weights_old)
        weights = updated.astype(bf)
        ours = pick((weights[:, :w], weights[:, w:]), me_half)
        theirs = swap(pick((weights[:, w:], weights[:, :w]), me_half))
        block = jnp.stack([pick((ours, theirs), me_half), pick((theirs, ours), me_half)], 0)
        gathered = jnp.concatenate([b.reshape(2 * shard, w) for b in gather_ring(block)], 0)
        produced = jnp.dot(upcoming, gathered, preferred_element_type=f32).astype(bf)
        ours = produced[:next_rows]
        theirs = swap(produced[next_rows:])
        outs.append(
            jnp.concatenate([pick((ours, theirs), me_half), pick((theirs, ours), me_half)], 1)
        )
        new_master.append(updated)
        new_one.append(first.astype(bf))
        new_two.append(second.astype(bf))
        begin += 2 * w

    def join(pieces):
        return jnp.concatenate(pieces, axis=1)[None]

    return join(new_master), join(new_one), join(new_two), join(outs)


def solution(mesh):
    fine = Mesh(mesh.devices.reshape(4, 2, 2, 2, 8), EXPERT + ("yl", "z"))
    both = P(EXPERT, ("yl", "z"), None)
    rows = P(EXPERT, ("yl", "z"), None, None)
    return jax.shard_map(
        per_device,
        mesh=fine,
        in_specs=(both, both, both, rows, rows, P(), both),
        out_specs=(both, both, both, both),
        check_vma=False,
    )
```

```python
import jax
import jax.numpy as jnp
from jax import lax
from jax.sharding import Mesh, PartitionSpec as P

CHUNKS = (5, 5, 4)

learn_rate = 0.002
beta_first = 0.9
beta_second = 0.95
epsilon = 1e-08
decay_rate = 0.1
correct_first = 1.0 - 0.9**10
correct_second = 1.0 - 0.95**10

EXPERT = ("x", "yh", "core")
RING = 8
ACROSS = [(i, (i + 1) % RING) for i in range(RING)]
ACROSS += [(RING + i, RING + (i - 1) % RING) for i in range(RING)]
SWAP = [(0, 1), (1, 0)]
RIGHT = [(i, (i + 1) % RING) for i in range(RING)]
LEFT = [(i, (i - 1) % RING) for i in range(RING)]


def swap(value):
    return lax.ppermute(value, "yl", SWAP)


def to_right(value):
    return lax.ppermute(value, "z", RIGHT)


def to_left(value):
    return lax.ppermute(value, "z", LEFT)


def rolled(value, axis, shift):
    twice = jnp.concatenate([value, value], axis=axis)
    return lax.dynamic_slice_in_dim(twice, shift, RING, axis)


def across(value):
    return lax.ppermute(value, ("core", "z"), ACROSS)


def pick(pair, which):
    return jnp.where(which == 0, pair[0], pair[1])


def reduce_ring(blocks):
    half = blocks.dtype
    bf = jnp.bfloat16
    right = to_right(blocks[4][:1].astype(bf))
    left = to_left(blocks[4][1:].astype(bf))
    f = jnp.float32
    right = to_right(
        jnp.concatenate([blocks[3][:1] + right.astype(f), blocks[3][1:]], 0).astype(bf)
    )
    left = to_left(
        jnp.concatenate([blocks[5][:1], blocks[5][1:] + left.astype(f)], 0).astype(bf)
    )
    for step in (2, 1):
        right = to_right((blocks[step] + right.astype(f)).astype(bf))
        left = to_left((blocks[8 - step] + left.astype(f)).astype(bf))
    return blocks[0] + (right.astype(f) + left.astype(f))


def gather_ring(block, me_core):
    right = [block]
    left = [block]
    for _ in range(3):
        right.append(to_right(right[-1]))
        left.append(to_left(left[-1]))
    far = across(pick((right[-1], left[-1]), me_core))
    return [block, left[1], left[2], left[3], far, right[3], right[2], right[1]]


def per_device(master, moment_one, moment_two, hidden_saved, out_grad, counts, next_hidden):
    bf = jnp.bfloat16
    f32 = jnp.float32
    me_expert = lax.axis_index(EXPERT)
    me_half = lax.axis_index("yl")
    me_z = lax.axis_index("z")
    me_core = lax.axis_index("core")
    experts = counts.shape[0]
    rows = hidden_saved.shape[2]
    slots = rows // experts
    ff = hidden_saved.shape[3]
    shard = master.shape[1]

    hidden = hidden_saved[0, 0]
    other = swap(hidden)
    loads = lax.dynamic_index_in_dim(counts, me_expert, 2, keepdims=False)
    loads = loads.reshape(experts, 2, RING)
    loads = lax.dynamic_index_in_dim(loads, me_z, 2, keepdims=False).T
    live = jnp.arange(slots, dtype=jnp.int32)[None, None, :] < loads[:, :, None]
    both = jnp.concatenate([pick((hidden, other), me_half), pick((other, hidden), me_half)], 0)
    both = jnp.where(live.reshape(2 * rows, 1), both, jnp.zeros_like(both))
    turned = both.T.reshape(2, RING, shard, 2 * rows)
    turned = rolled(turned, 1, me_z).swapaxes(0, 1).reshape(ff, 2 * rows)

    mine = next_hidden[0]
    upcoming = jnp.concatenate([mine, swap(mine)], 0)
    next_rows = mine.shape[0]
    upcoming = upcoming.reshape(2 * next_rows, 2, RING, shard)
    upcoming = rolled(upcoming, 2, me_z).swapaxes(1, 2).reshape(2 * next_rows, ff)

    grads = out_grad[0, 0]
    new_master, new_one, new_two, outs = [], [], [], []
    begin = 0
    for tiles in CHUNKS:
        w = tiles * 128
        cols = slice(begin, begin + 2 * w)
        part = grads[:, cols].reshape(rows, 2, w).swapaxes(0, 1)
        part = part.reshape(2 * experts, slots, w)
        arrived = lax.all_to_all(part, ("yl",) + EXPERT, 0, 0).reshape(2 * rows, w)
        product = jnp.dot(turned, arrived, preferred_element_type=f32)
        total = reduce_ring(product.astype(bf).astype(f32).reshape(RING, 2, shard, w))
        theirs = swap(pick((total[1], total[0]), me_half).astype(bf)).astype(f32)
        ours = pick((total[0], total[1]), me_half)
        gradient = jnp.concatenate(
            [pick((ours, theirs), me_half), pick((theirs, ours), me_half)], 1
        )
        weights_old = master[0, :, cols]
        first = beta_first * moment_one[0, :, cols].astype(f32) + (1.0 - beta_first) * gradient
        second = (
            beta_second * moment_two[0, :, cols].astype(f32)
            + (1.0 - beta_second) * gradient * gradient
        )
        step_size = first / correct_first / (jnp.sqrt(second / correct_second) + epsilon)
        updated = weights_old - learn_rate * (step_size + decay_rate * weights_old)
        weights = updated.astype(bf)
        ours = pick((weights[:, :w], weights[:, w:]), me_half)
        theirs = swap(pick((weights[:, w:], weights[:, :w]), me_half))
        block = jnp.stack([pick((ours, theirs), me_half), pick((theirs, ours), me_half)], 0)
        gathered = jnp.concatenate([b.reshape(2 * shard, w) for b in gather_ring(block, me_core)], 0)
        produced = jnp.dot(upcoming, gathered, preferred_element_type=f32).astype(bf)
        ours = produced[:next_rows]
        theirs = swap(produced[next_rows:])
        outs.append(
            jnp.concatenate([pick((ours, theirs), me_half), pick((theirs, ours), me_half)], 1)
        )
        new_master.append(updated)
        new_one.append(first.astype(bf))
        new_two.append(second.astype(bf))
        begin += 2 * w

    def join(pieces):
        return jnp.concatenate(pieces, axis=1)[None]

    return join(new_master), join(new_one), join(new_two), join(outs)


def solution(mesh):
    fine = Mesh(mesh.devices.reshape(4, 2, 2, 2, 8), EXPERT + ("yl", "z"))
    both = P(EXPERT, ("yl", "z"), None)
    rows = P(EXPERT, ("yl", "z"), None, None)
    return jax.shard_map(
        per_device,
        mesh=fine,
        in_specs=(both, both, both, rows, rows, P(), both),
        out_specs=(both, both, both, both),
        check_vma=False,
    )
```

```python
import jax
import jax.numpy as jnp
from jax import lax
from jax.sharding import Mesh, PartitionSpec as P

CHUNKS = ((5, 5), (4,))

learn_rate = 0.002
beta_first = 0.9
beta_second = 0.95
epsilon = 1e-08
decay_rate = 0.1
correct_first = 1.0 - 0.9**10
correct_second = 1.0 - 0.95**10

EXPERT = ("x", "yh", "core")
RING = 8
SWAP = [(0, 1), (1, 0)]
RIGHT = [(i, (i + 1) % RING) for i in range(RING)]
LEFT = [(i, (i - 1) % RING) for i in range(RING)]


def swap(value):
    return lax.ppermute(value, "yl", SWAP)


def to_right(value):
    return lax.ppermute(value, "z", RIGHT)


def to_left(value):
    return lax.ppermute(value, "z", LEFT)


def rolled(value, axis, shift):
    twice = jnp.concatenate([value, value], axis=axis)
    return lax.dynamic_slice_in_dim(twice, shift, RING, axis)


def pick(pair, which):
    return jnp.where(which == 0, pair[0], pair[1])


def reduce_ring(blocks):
    half = blocks.dtype
    bf = jnp.bfloat16
    right = to_right(blocks[4][:1].astype(bf))
    left = to_left(blocks[4][1:].astype(bf))
    f = jnp.float32
    right = to_right(
        jnp.concatenate([blocks[3][:1] + right.astype(f), blocks[3][1:]], 0).astype(bf)
    )
    left = to_left(
        jnp.concatenate([blocks[5][:1], blocks[5][1:] + left.astype(f)], 0).astype(bf)
    )
    for step in (2, 1):
        right = to_right((blocks[step] + right.astype(f)).astype(bf))
        left = to_left((blocks[8 - step] + left.astype(f)).astype(bf))
    return blocks[0] + (right.astype(f) + left.astype(f))


def gather_ring(block):
    right = [block]
    left = [block]
    for _ in range(3):
        right.append(to_right(right[-1]))
        left.append(to_left(left[-1]))
    far = jnp.concatenate([to_right(right[-1][:1]), to_left(left[-1][1:])], 0)
    return [block, left[1], left[2], left[3], far, right[3], right[2], right[1]]


def per_device(master, moment_one, moment_two, hidden_saved, out_grad, counts, next_hidden):
    bf = jnp.bfloat16
    f32 = jnp.float32
    me_expert = lax.axis_index(EXPERT)
    me_half = lax.axis_index("yl")
    me_z = lax.axis_index("z")
    experts = counts.shape[0]
    rows = hidden_saved.shape[2]
    slots = rows // experts
    ff = hidden_saved.shape[3]
    shard = master.shape[1]

    hidden = hidden_saved[0, 0]
    other = swap(hidden)
    loads = lax.dynamic_index_in_dim(counts, me_expert, 2, keepdims=False)
    loads = loads.reshape(experts, 2, RING)
    loads = lax.dynamic_index_in_dim(loads, me_z, 2, keepdims=False).T
    live = jnp.arange(slots, dtype=jnp.int32)[None, None, :] < loads[:, :, None]
    both = jnp.concatenate([pick((hidden, other), me_half), pick((other, hidden), me_half)], 0)
    both = jnp.where(live.reshape(2 * rows, 1), both, jnp.zeros_like(both))
    turned = both.T.reshape(2, RING, shard, 2 * rows)
    turned = rolled(turned, 1, me_z).swapaxes(0, 1).reshape(ff, 2 * rows)

    mine = next_hidden[0]
    upcoming = jnp.concatenate([mine, swap(mine)], 0)
    next_rows = mine.shape[0]
    upcoming = upcoming.reshape(2 * next_rows, 2, RING, shard)
    upcoming = rolled(upcoming, 2, me_z).swapaxes(1, 2).reshape(2 * next_rows, ff)

    grads = out_grad[0, 0]
    new_master, new_one, new_two, outs = [], [], [], []
    begin = 0
    for tiles in CHUNKS:
        w = sum(tiles) * 128
        cols = slice(begin, begin + 2 * w)
        products = []
        inner = begin
        for piece in tiles:
            n = piece * 128
            part = jnp.stack([grads[:, inner : inner + n], grads[:, inner + w : inner + w + n]])
            part = part.reshape(2 * experts, slots, n)
            arrived = lax.all_to_all(part, ("yl",) + EXPERT, 0, 0).reshape(2 * rows, n)
            products.append(jnp.dot(turned, arrived, preferred_element_type=f32))
            inner += n
        product = jnp.concatenate(products, axis=1)
        total = reduce_ring(product.reshape(RING, 2, shard, w))
        theirs = swap(pick((total[1], total[0]), me_half).astype(bf)).astype(f32)
        ours = pick((total[0], total[1]), me_half)
        gradient = jnp.concatenate(
            [pick((ours, theirs), me_half), pick((theirs, ours), me_half)], 1
        )
        weights_old = master[0, :, cols]
        first = beta_first * moment_one[0, :, cols].astype(f32) + (1.0 - beta_first) * gradient
        second = (
            beta_second * moment_two[0, :, cols].astype(f32)
            + (1.0 - beta_second) * gradient * gradient
        )
        step_size = first / correct_first / (jnp.sqrt(second / correct_second) + epsilon)
        updated = weights_old - learn_rate * (step_size + decay_rate * weights_old)
        weights = updated.astype(bf)
        ours = pick((weights[:, :w], weights[:, w:]), me_half)
        theirs = swap(pick((weights[:, w:], weights[:, :w]), me_half))
        block = jnp.stack([pick((ours, theirs), me_half), pick((theirs, ours), me_half)], 0)
        gathered = jnp.concatenate([b.reshape(2 * shard, w) for b in gather_ring(block)], 0)
        produced = jnp.dot(upcoming, gathered, preferred_element_type=f32).astype(bf)
        ours = produced[:next_rows]
        theirs = swap(produced[next_rows:])
        outs.append(
            jnp.concatenate([pick((ours, theirs), me_half), pick((theirs, ours), me_half)], 1)
        )
        new_master.append(updated)
        new_one.append(first.astype(bf))
        new_two.append(second.astype(bf))
        begin += 2 * w

    def join(pieces):
        return jnp.concatenate(pieces, axis=1)[None]

    return join(new_master), join(new_one), join(new_two), join(outs)


def solution(mesh):
    fine = Mesh(mesh.devices.reshape(4, 2, 2, 2, 8), EXPERT + ("yl", "z"))
    both = P(EXPERT, ("yl", "z"), None)
    rows = P(EXPERT, ("yl", "z"), None, None)
    return jax.shard_map(
        per_device,
        mesh=fine,
        in_specs=(both, both, both, rows, rows, P(), both),
        out_specs=(both, both, both, both),
        check_vma=False,
    )
```
